32 devices in a mesh: dp: 8 (over y, x, core), tensor: 4 (over z).
Axes of the slice: x: 2, y: 2, z: 4, core: 2. Of those that a mesh axis runs over, the one named last changes fastest.
Arguments:
- tokens: bfloat16 [6144, 2048], P('dp'), may hold values from -6 to 6
- targets: bfloat16 [6144, 2048], P('dp'), may hold values from -6 to 6
- up_weight: bfloat16 [8, 64, 256, 256], P('dp', 'tensor'), may hold values from -6 to 6
- down_weight: bfloat16 [8, 64, 256, 256], P('dp', 'tensor'), may hold values from -6 to 6
- block_rows: int32 [64], P('tensor'), may hold values from 0 to 7, as said below
- block_columns: int32 [64], P('tensor'), may hold values from 0 to 7, as said below
Outputs:
- new_up: bfloat16 [8, 64, 256, 256], P('dp', 'tensor')
- new_down: bfloat16 [8, 64, 256, 256], P('dp', 'tensor')
- input_grad: bfloat16 [6144, 2048], P('dp', 'tensor')
The draws below stay inside these ranges and needn't reach their ends.
Inputs may be any that keep to these rules, and one draw needn't show every extreme that they name: Within each tensor shard the 16 blocks sit at distinct (block_rows, block_columns) positions, and every hidden block of a shard holds exactly 2 of them; up_weight and down_weight share this pattern. `block_columns`: hidden block indices within a shard.
All inputs are finite; a program needn't handle non-finite values.
Results may differ from the reference program's by a relative error of at most 0.015.
Values may be sent and summed in bfloat16 or wider, within the bound.
No kernel may reach another device: no remote copies, remote signals or barrier semaphores. Data moves between devices by JAX's collectives and lax.ppermute only.
A program may use at most 128 MiB of HBM per device.

```python
import jax
import jax.numpy as jnp
from jax import lax

D = 2048
H = 8192
BLK = 256
TOK = 768
BLOCKS = 16
N_DP = 8
N_TENSOR = 4


def pattern_pair(key):
    model_blocks = D // BLK
    shard_hidden = H // (N_TENSOR * BLK)
    per_column = model_blocks // 4

    def one_shard(shard_key):
        row_perm = jax.random.permutation(jax.random.fold_in(shard_key, 1), model_blocks)
        col_shift = jax.random.permutation(jax.random.fold_in(shard_key, 2), shard_hidden)
        order = jax.random.permutation(jax.random.fold_in(shard_key, 3), shard_hidden * per_column)
        col_ids = jnp.repeat(jnp.arange(shard_hidden), per_column)
        offsets = jnp.tile(jnp.arange(per_column), shard_hidden) * 4
        rows = row_perm[(col_shift[col_ids] + offsets) % model_blocks]
        return (rows[order].astype(jnp.int32), col_ids[order].astype(jnp.int32))
    keys = jax.random.split(jax.random.fold_in(key, 11), N_TENSOR)
    rows, cols = jax.vmap(one_shard)(keys)
    return (rows.reshape(-1), cols.reshape(-1))


def draw_block_rows(key, part):
    return pattern_pair(key)[0]


def draw_block_columns(key, part):
    return pattern_pair(key)[1]


def levels(stream_key, extent, cuts, low, largest):
    gain = 1.0
    for position, blocks in cuts:
        steps = jax.random.uniform(jax.random.fold_in(jax.random.fold_in(stream_key, 6), position), (blocks,), jnp.float32, low / len(cuts), largest / len(cuts))
        gain = gain * jnp.repeat(jnp.exp(steps), extent[position] // blocks).reshape((-1,) + (1,) * (len(extent) - 1 - position))
    return gain


def bell_draw(own_key, shape, spread, most, shards=(), held_as=jnp.bfloat16):
    entries = spread * jax.random.normal(own_key, shape, jnp.float32)
    if shards:
        entries = entries * levels(own_key, shape, shards, -0.22, 0.18)
    return jnp.clip(entries, -most, most).astype(held_as)


def setup_inputs(seed: int = 0) -> dict:
    streams_of = jax.random.split(jax.random.key(seed), 7)
    tokens = bell_draw(streams_of[0], (N_DP * TOK, D), 1.0, 6.0, ((0, 8),))
    targets = bell_draw(streams_of[1], (N_DP * TOK, D), 1.0, 6.0, ((0, 8),))
    up_weight = bell_draw(streams_of[2], (N_DP, N_TENSOR * BLOCKS, BLK, BLK), 1.0, 6.0, ((0, 8), (1, 4)))
    down_weight = bell_draw(streams_of[3], (N_DP, N_TENSOR * BLOCKS, BLK, BLK), 1.0, 6.0, ((0, 8), (1, 4)))
    block_rows = draw_block_rows(jax.random.fold_in(streams_of[6], 71), 0)
    block_columns = draw_block_columns(jax.random.fold_in(streams_of[6], 71), 0)
    return dict(tokens=tokens, targets=targets, up_weight=up_weight, down_weight=down_weight, block_rows=block_rows, block_columns=block_columns)


step_rate = 0.5


def replica_step(tok_rows, target_rows, up_mine, down_mine, up_peer, down_peer, block_rows, block_columns):
    model_blocks = D // BLK
    shard_hidden = H // (N_TENSOR * BLK)
    hidden_blocks = shard_hidden * N_TENSOR
    total_blocks = N_TENSOR * BLOCKS
    scale_in = (D // 4) ** -0.5
    scale_out = (H // 4) ** -0.5
    shard_of = (jnp.arange(total_blocks) // BLOCKS).astype(jnp.int32)
    global_cols = (shard_of * shard_hidden + block_columns).astype(jnp.int32)
    row_ids = (shard_of * model_blocks + block_rows).astype(jnp.int32)
    up_float = up_mine.astype(jnp.float32)
    down_float = down_mine.astype(jnp.float32)
    tok_blocks = jnp.transpose(tok_rows.reshape(TOK, model_blocks, BLK)[:, block_rows, :], (1, 0, 2)).astype(jnp.float32)
    first = jnp.einsum("ntk,nkj->ntj", tok_blocks, up_float)
    hidden_pre = jax.ops.segment_sum(first, global_cols, num_segments=hidden_blocks) * scale_in
    active = jax.nn.silu(hidden_pre).astype(jnp.bfloat16)
    active_blocks = active[global_cols].astype(jnp.float32)
    second = jnp.einsum("ntj,njk->ntk", active_blocks, down_float)
    out_parts = (jax.ops.segment_sum(second, row_ids, num_segments=N_TENSOR * model_blocks) * scale_out).astype(jnp.bfloat16)
    out_parts = lax.optimization_barrier(out_parts)
    out_sum = out_parts.astype(jnp.float32).reshape(N_TENSOR, model_blocks, TOK, BLK).sum(0)
    output = jnp.transpose(out_sum, (1, 0, 2)).reshape(TOK, D)
    error = (output - target_rows.astype(jnp.float32)).astype(jnp.bfloat16)
    error_blocks = jnp.transpose(error.reshape(TOK, model_blocks, BLK)[:, block_rows, :], (1, 0, 2)).astype(jnp.float32)
    grad_down = scale_out * jnp.einsum("ntj,ntk->njk", active_blocks, error_blocks)
    dact_blocks = jnp.einsum("ntk,njk->ntj", error_blocks, down_float)
    dact = jax.ops.segment_sum(dact_blocks, global_cols, num_segments=hidden_blocks) * scale_out
    sigma = jax.nn.sigmoid(hidden_pre)
    dpre = (dact * sigma * (1.0 + hidden_pre * (1.0 - sigma))).astype(jnp.bfloat16)
    dpre_blocks = dpre[global_cols].astype(jnp.float32)
    grad_up = scale_in * jnp.einsum("ntk,ntj->nkj", tok_blocks, dpre_blocks)
    back_blocks = jnp.einsum("ntj,nkj->ntk", dpre_blocks, up_float)
    back_parts = (jax.ops.segment_sum(back_blocks, row_ids, num_segments=N_TENSOR * model_blocks) * scale_in).astype(jnp.bfloat16)
    back_parts = lax.optimization_barrier(back_parts)
    back_sum = back_parts.astype(jnp.float32).reshape(N_TENSOR, model_blocks, TOK, BLK).sum(0)
    input_grad = jnp.transpose(back_sum, (1, 0, 2)).reshape(TOK, D).astype(jnp.bfloat16)
    new_up = (0.5 * (up_float + up_peer.astype(jnp.float32)) - step_rate * grad_up).astype(jnp.bfloat16)
    new_down = (0.5 * (down_float + down_peer.astype(jnp.float32)) - step_rate * grad_down).astype(jnp.bfloat16)
    return new_up, new_down, input_grad


def reference(tokens, targets, up_weight, down_weight, block_rows, block_columns):
    level = (N_DP.bit_length() - 1) // 2
    tok_all = tokens.reshape(N_DP, TOK, D)
    target_all = targets.reshape(N_DP, TOK, D)

    def one_replica(replica):
        partner = jnp.bitwise_xor(replica, jnp.int32(1 << level)).astype(jnp.int32)
        return replica_step(tok_all[replica], target_all[replica], up_weight[replica], down_weight[replica],
                            up_weight[partner], down_weight[partner], block_rows, block_columns)

    new_up, new_down, input_grad = lax.map(one_replica, jnp.arange(N_DP, dtype=jnp.int32))
    return new_up, new_down, input_grad.reshape(N_DP * TOK, D)
```

```python
import functools

import jax
import jax.numpy as jnp
from jax import lax
from jax.experimental import pallas as pl
from jax.experimental.pallas import tpu as pltpu
from jax.sharding import PartitionSpec as P

step_rate = 0.5
per_column = 2
ANY = pl.BlockSpec(memory_space=pltpu.HBM)
ANYV = pl.BlockSpec(memory_space=pltpu.VMEM)
SMEM = pl.BlockSpec(memory_space=pltpu.SMEM)
f32 = jnp.float32
bf16 = jnp.bfloat16
NT = (((1,), (1,)), ((), ()))
TN = (((0,), (0,)), ((), ()))


def params(mib=20):
    return pltpu.CompilerParams(vmem_limit_bytes=mib << 20)


def cost(flops, nbytes):
    return pl.CostEstimate(flops=1, bytes_accessed=1, transcendentals=0)


def lanes(index, size):
    return pl.ds(pl.multiple_of(index * size, size), size)


def column_table(cols_ref, table, count, blocks):
    for h in range(blocks // per_column):
        count[h] = 0
    for k in range(blocks):
        h = cols_ref[k]
        seen = count[h]
        table[per_column * h + seen] = k
        count[h] = seen + 1


def forward_kernel(start, scale_in, scale_out, direct, first, rows_ref, cols_ref, tok_hbm, up, down, dep, also, *refs):
    if first:
        up_hbm, down_hbm = up, down
        (part, act, fac, up, down), refs = refs[:5], refs[5:]
    else:
        (part, act, fac), refs = refs[2:5], refs[5:]
    outs, token, (tok, acc, table, count, sems), refs = refs[:direct], refs[direct], refs[direct + 1:direct + 6], refs[direct + 6:]
    size, width = tok.shape
    blocks, blk = up.shape[0], up.shape[1]
    mine = pl.ds(start, size)
    copies = [pltpu.make_async_copy(tok_hbm.at[mine], tok, sems.at[0])]
    if first:
        small = [pltpu.make_async_copy(rows_ref, refs[0], sems.at[1]), pltpu.make_async_copy(cols_ref, refs[1], sems.at[2])]
        rows_ref, cols_ref = refs
        copies += small
    for c in copies:
        c.start()
    if first:
        ups = [pltpu.make_async_copy(up_hbm.at[k], up.at[k], sems.at[3]) for k in range(blocks)]
        downs = [pltpu.make_async_copy(down_hbm.at[k], down.at[k], sems.at[4]) for k in range(blocks)]
        for c in ups + downs:
            c.start()
    acc[...] = jnp.zeros_like(acc)
    for c in copies[1:]:
        c.wait()
    column_table(cols_ref, table, count, blocks)
    copies[0].wait()
    if first:
        for c in ups:
            c.wait()
    for h in range(blocks // per_column):
        pre = None
        for j in range(per_column):
            k = table[per_column * h + j]
            term = jnp.dot(tok[:, lanes(rows_ref[k], blk)], up[k], preferred_element_type=f32)
            pre = term if pre is None else pre + term
        pre = pre * scale_in
        sig = 1.0 / (1.0 + jnp.exp(-pre))
        act[mine, h * blk:(h + 1) * blk] = (pre * sig).astype(bf16)
        fac[mine, h * blk:(h + 1) * blk] = (sig * (1.0 + pre * (1.0 - sig)) * scale_out).astype(bf16)
    if first:
        for c in downs:
            c.wait()
    for k in range(blocks):
        r = rows_ref[k]
        acc[r] += jnp.dot(act[mine, lanes(cols_ref[k], blk)], down[k], preferred_element_type=f32)
    for b in range(acc.shape[0]):
        part[:, b * blk:(b + 1) * blk] = (acc[b] * scale_out).astype(bf16)
    for c in shares_of(part, outs, sems.at[5]):
        c.wait()


def shares_of(whole, outs, sem):
    if not outs:
        return []
    share = whole.shape[1] // (len(outs) + 1)
    place = lax.axis_index("tensor")
    copies = [pltpu.make_async_copy(whole.at[:, lanes(place ^ (i + 1), share)], out, sem) for i, out in enumerate(outs)]
    for c in copies:
        c.start()
    return copies


def backward_kernel(start, sizes, terms, ready, direct, first, scale_in, rows_ref, cols_ref, *refs):
    parts, refs = refs[:terms * len(sizes)], refs[terms * len(sizes):]
    (tgt_hbm, fac, up, down, dep, also), refs = refs[:6], refs[6 if first else 8:]
    (back, send, err, dpre), outs, refs = refs[:4], refs[4:4 + direct], refs[5 + direct:]
    tgt, acc, table, count, sems = refs
    size, width = tgt.shape
    blocks, blk = up.shape[0], up.shape[1]
    mine = pl.ds(start, size)
    place = lax.axis_index("tensor")
    if not ready:
        copy = pltpu.make_async_copy(tgt_hbm.at[mine], tgt, sems.at[0])
        copy.start()
    column_table(cols_ref, table, count, blocks)
    acc[...] = jnp.zeros_like(acc)
    share = width // terms
    if ready:
        copies, offset = [], start
        for n, rows in enumerate(sizes):
            for i in range(terms):
                target = err.at[pl.ds(offset, rows), lanes(place ^ i, share)]
                copies.append(pltpu.make_async_copy(parts[n * terms + i], target, sems.at[0]))
                copies[-1].start()
            offset += rows
        for c in copies:
            c.wait()
    else:
        copy.wait()
        offset = 0
        for n, rows in enumerate(sizes):
            for b in range(width // blk):
                s = slice(b * blk, (b + 1) * blk)
                total = parts[n * terms][:, s].astype(f32)
                for i in range(1, terms):
                    total += parts[n * terms + i][:, s].astype(f32)
                err[pl.ds(start + offset, rows), s] = (total - tgt[pl.ds(offset, rows), s].astype(f32)).astype(bf16)
            offset += rows
    for h in range(blocks // per_column):
        dact = None
        for j in range(per_column):
            k = table[per_column * h + j]
            term = lax.dot_general(err[mine, lanes(rows_ref[k], blk)], down[k], NT, preferred_element_type=f32)
            dact = term if dact is None else dact + term
        s = slice(h * blk, (h + 1) * blk)
        dpre[mine, s] = (dact * fac[mine, s].astype(f32)).astype(bf16)
    for k in range(blocks):
        r = rows_ref[k]
        acc[r] += lax.dot_general(dpre[mine, lanes(cols_ref[k], blk)], up[k], NT, preferred_element_type=f32)
    for b in range(acc.shape[0]):
        back[:, b * blk:(b + 1) * blk] = (acc[b] * scale_in).astype(bf16)
    out = shares_of(back, outs, sems.at[1])
    if not direct and terms > 1:
        first_column = jnp.where(place == 0, share, 0)
        copy = pltpu.make_async_copy(back.at[:, pl.ds(pl.multiple_of(first_column, share), width - share)], send, sems.at[1])
        copy.start()
        out.append(copy)
    for c in out:
        c.wait()


def error_kernel(start, count, *refs):
    terms, (tgt_hbm, dep, also, o_ref, token, tgt, sem) = refs[:count], refs[count:]
    size, share = tgt.shape
    own = lanes(lax.axis_index("tensor"), share)
    copy = pltpu.make_async_copy(tgt_hbm.at[pl.ds(start, size), own], tgt, sem)
    copy.start()
    total = terms[0][:, own].astype(f32)
    for i in range(1, count):
        total += terms[i][...].astype(f32)
    copy.wait()
    o_ref[...] = (total - tgt[...].astype(f32)).astype(bf16)


def add_kernel(a_ref, b_ref, dep, also, o_ref, token):
    o_ref[...] = (a_ref[...].astype(f32) + b_ref[...].astype(f32)).astype(bf16)


def pass_on_kernel(hop, count, back, got, dep, also, o_ref, token):
    width = o_ref.shape[1]
    part = width // (count - hop)
    right = lax.axis_index("tensor") == hop - 1
    a = back[:, pl.ds(pl.multiple_of(jnp.where(right, hop * part, 0), part), width)]
    b = got[:, pl.ds(pl.multiple_of(jnp.where(right, part, 0), part), width)]
    o_ref[...] = (a.astype(f32) + b.astype(f32)).astype(bf16)


def finish_kernel(start, count, direct, *refs):
    terms, (old, dep, also, out_hbm, token, buf, sem) = refs[:count], refs[count:]
    size, part = buf.shape
    place = lax.axis_index("tensor")
    total = terms[0][:, lanes(place, part)].astype(f32)
    for j in range(1, count):
        if direct:
            total += terms[j][...].astype(f32)
        else:
            at = jnp.where(place == j, 0, (count - 1 - j) * part)
            total += terms[j][:, pl.ds(pl.multiple_of(at, part), part)].astype(f32)
    buf[...] = total.astype(bf16)
    copy = pltpu.make_async_copy(buf, out_hbm.at[pl.ds(start, size)], sem)
    copy.start()
    copy.wait()


def turn_kernel(act, tok_hbm, dep, also, act_t, tok_t, token, tok, sems):
    count, blk = act_t.shape[0], act_t.shape[1]
    columns = [slice(b * blk, (b + 1) * blk) for b in range(count)]
    copies = [pltpu.make_async_copy(tok_hbm.at[:, c], tok.at[:, c], sems.at[b]) for b, c in enumerate(columns)]
    for c in copies:
        c.start()
    for b, c in enumerate(columns):
        act_t[b] = act[:, c].T
    for b, c in enumerate(columns):
        copies[b].wait()
        tok_t[b] = tok[:, c].T


def grad_kernel(scale, by_hidden, rows_ref, cols_ref, left, right, own, peer_hbm, dep, also, out_hbm, token,
                peer, out, table, count, sems):
    blocks, blk = own.shape[0], own.shape[1]
    copies = [pltpu.make_async_copy(peer_hbm.at[k], peer.at[k], sems.at[0]) for k in range(blocks)]
    for c in copies:
        c.start()
    column_table(cols_ref, table, count, blocks)
    for c in copies:
        c.wait()
    done = []
    for h in range(blocks // per_column):
        for j in range(per_column):
            k = table[per_column * h + j]
            model = rows_ref[k]
            if by_hidden:
                grad = jnp.dot(left[h], right[:, lanes(model, blk)], preferred_element_type=f32)
            else:
                grad = jnp.dot(left[model], right[:, h * blk:(h + 1) * blk], preferred_element_type=f32)
            mixed = 0.5 * (own[k].astype(f32) + peer[k].astype(f32))
            out[k] = (mixed - (step_rate * scale) * grad).astype(bf16)
            done.append(pltpu.make_async_copy(out.at[k], out_hbm.at[k], sems.at[1]))
            done[-1].start()
    for c in done:
        c.wait()


def cut(total, shares, unit=16):
    edges = [0]
    for i in range(1, len(shares)):
        edges.append(round(total * sum(shares[:i]) / sum(shares) / unit) * unit)
    edges.append(total)
    return [(a, b - a) for a, b in zip(edges, edges[1:]) if b > a]


def on_device(shares, groups, direct_sum, direct_grad, tokens, targets, up_weight, down_weight, block_rows, block_columns):
    tok_count, width = tokens.shape
    up, down = up_weight[0], down_weight[0]
    blocks, blk = up.shape[0], up.shape[1]
    count = lax.axis_size("tensor")
    hops = count - 1
    hidden = blocks // per_column * blk
    scale_in = (width // 4) ** -0.5
    scale_out = (hidden * count // 4) ** -0.5
    level = (lax.axis_size("dp").bit_length() - 1) // 2
    part = width // count
    model_blocks = width // blk

    def hop(x, j):
        return lax.ppermute(x, "tensor", [(j - 1, j), (count - j, count - 1 - j)])

    def across(x, k):
        return lax.ppermute(x, "tensor", [(i, i ^ k) for i in range(count)])

    def partner(x):
        return lax.ppermute(x, "dp", [(i, i ^ (1 << level)) for i in range(lax.axis_size("dp"))])

    peer_up, peer_down = partner(up), partner(down)
    chunks = cut(tok_count, shares)
    C = len(chunks)
    like = lambda *s: jax.ShapeDtypeStruct(s, bf16)
    V = lambda *s: pltpu.VMEM(s, bf16)

    state = dict(act=None, fac=None, err=None, dpre=None, out=None, dep=block_rows)
    part_of, back_of, new = {}, {}, {}
    got = {}
    gotg = {}

    token = pltpu.HBM((16, 128), bf16)
    in_hbm = lambda x: pltpu.with_memory_space_constraint(x, pltpu.HBM)
    in_vmem = lambda x: pltpu.with_memory_space_constraint(x, pltpu.VMEM)
    weights = lambda: (in_vmem(state["up"]), in_vmem(state["down"]))

    spans = [(chunks[g[0]][0], sum(chunks[c][1] for c in g)) for g in groups]

    def after():
        return in_hbm(state["dep"]), in_hbm(state.pop("also", state["dep"]))

    def forward(c):
        start, size = chunks[c]
        first = c == 0
        direct = hops if c in direct_sum else 0
        scratch = [V(size, width), pltpu.VMEM((model_blocks, size, blk), f32),
                   pltpu.SMEM((blocks,), jnp.int32), pltpu.SMEM((blocks // per_column,), jnp.int32),
                   pltpu.SemaphoreType.DMA((6,))]
        held = (V(tok_count, hidden), V(tok_count, hidden))
        if first:
            scratch += [pltpu.SMEM((blocks,), jnp.int32), pltpu.SMEM((blocks,), jnp.int32)]
            a = [in_hbm(x) for x in (block_rows, block_columns, tokens, up, down, block_rows, block_rows)]
            specs, alias = [ANY] * 7, {}
            held += (V(*up.shape), V(*down.shape))
        else:
            a = [block_rows, block_columns, in_hbm(tokens), *weights(), *after(), in_vmem(state["act"]), in_vmem(state["fac"])]
            specs, alias = [SMEM, SMEM, ANY, ANYV, ANYV, ANY, ANY, ANYV, ANYV], {7: 1, 8: 2}
        p, act, fac, *outs = pl.pallas_call(
            functools.partial(forward_kernel, start, scale_in, scale_out, direct, first),
            out_shape=(V(size, width), *held) + (like(size, part),) * direct + (token,),
            in_specs=specs, out_specs=(ANYV,) * (1 + len(held) + direct) + (ANY,),
            input_output_aliases=alias, scratch_shapes=scratch,
            compiler_params=params(), name=f"forward_{c}", cost_estimate=cost(1, 1),
        )(*a)
        if first:
            state.update(up=outs.pop(0), down=outs.pop(0))
        *sends, done = outs
        state.update(act=act, fac=fac, dep=done)
        part_of[c] = p
        if direct:
            for i, x in enumerate(sends):
                got[c, i + 1] = across(x, i + 1)
        elif hops:
            got[c, 1] = hop(p, 1)

    def error(c):
        start, size = chunks[c]
        e, done = pl.pallas_call(
            functools.partial(error_kernel, start, count), out_shape=(like(size, part), token),
            in_specs=[ANYV] * count + [ANY] * 3, out_specs=(ANYV, ANY),
            scratch_shapes=[V(size, part), pltpu.SemaphoreType.DMA],
            compiler_params=params(), name=f"error_{c}", cost_estimate=cost(1, 1),
        )(part_of[c], *[got[c, i] for i in range(1, count)], in_hbm(targets), *after())
        state["dep"] = done
        got[c, 0] = e
        for i in range(1, count):
            got[c, i] = across(e, i)

    def add(c, j):
        start, size = chunks[c]
        s, done = pl.pallas_call(
            add_kernel, out_shape=(like(size, width), token),
            in_specs=[ANYV, ANYV, ANY, ANY], out_specs=(ANYV, ANY),
            compiler_params=params(), name=f"add_{c}_{j}", cost_estimate=cost(1, 1),
        )(part_of[c], got[c, j - 1], *after())
        state["dep"] = done
        got[c, j] = hop(s, j)

    def backward(c):
        start, size = spans[c]
        first = c == 0
        ready = groups[c][0] in direct_sum
        direct = hops if c in direct_grad else 0
        a = [block_rows, block_columns]
        for n in groups[c]:
            a += [got[n, 0] if ready else part_of[n]] + [got[n, j] for j in range(1, count)]
        a += [in_hbm(targets), in_vmem(state["fac"]), *weights(), *after()]
        specs = [SMEM, SMEM] + [ANYV] * (count * len(groups[c])) + [ANY] + [ANYV] * 3 + [ANY] * 2
        alias = {}
        if not first:
            alias = {len(a): 2, len(a) + 1: 3}
            a += [in_vmem(state["err"]), in_vmem(state["dpre"])]
            specs += [ANYV] * 2
        chain = like(size, width - part) if hops and not direct else like(16, 128)
        g, send, err, dpre, *sends, done = pl.pallas_call(
            functools.partial(backward_kernel, start, [chunks[n][1] for n in groups[c]], count, ready, direct, first, scale_in),
            out_shape=(V(size, width), chain, V(tok_count, width), V(tok_count, hidden)) + (like(size, part),) * direct + (token,),
            in_specs=specs, out_specs=(ANYV,) * (4 + direct) + (ANY,),
            input_output_aliases=alias,
            scratch_shapes=[V(size, width), pltpu.VMEM((model_blocks, size, blk), f32),
                            pltpu.SMEM((blocks,), jnp.int32), pltpu.SMEM((blocks // per_column,), jnp.int32),
                            pltpu.SemaphoreType.DMA((2,))],
            compiler_params=params(), name=f"backward_{c}", cost_estimate=cost(1, 1),
        )(*a)
        state.update(err=err, dpre=dpre, dep=done)
        back_of[c] = g
        if direct:
            for i, x in enumerate(sends):
                gotg[c, i + 1] = across(x, i + 1)
        elif hops:
            gotg[c, 1] = hop(send, 1)

    def pass_on(c, j):
        start, size = spans[c]
        wide = (count - j) * part
        s, done = pl.pallas_call(
            functools.partial(pass_on_kernel, j, count), out_shape=(like(size, wide), token),
            in_specs=[ANYV, ANYV, ANY, ANY], out_specs=(ANYV, ANY),
            compiler_params=params(), name=f"pass_on_{c}_{j}", cost_estimate=cost(1, 1),
        )(back_of[c], gotg[c, j - 1], *after())
        state["dep"] = done
        gotg[c, j] = hop(s, j)

    def finish(c):
        start, size = spans[c]
        first = state["out"] is None
        a = [back_of[c]] + [gotg[c, j] for j in range(1, count)] + [tokens if first else state["out"], *after()]
        o, done = pl.pallas_call(
            functools.partial(finish_kernel, start, count, c in direct_grad), out_shape=(like(tok_count, part), token),
            in_specs=[ANYV] * count + [ANY] * 3, out_specs=(ANY, ANY),
            input_output_aliases={} if first else {count: 0},
            scratch_shapes=[V(size, part), pltpu.SemaphoreType.DMA],
            compiler_params=params(), name=f"finish_{c}", cost_estimate=cost(size * width, 5 * size * width),
        )(*a)
        state.update(out=o, dep=done)

    def turn():
        turned = V(model_blocks, blk, tok_count)
        act_t, tok_t, done = pl.pallas_call(
            turn_kernel, out_shape=(turned, turned, token), in_specs=[ANYV] + [ANY] * 3, out_specs=(ANYV, ANYV, ANY),
            scratch_shapes=[V(tok_count, width), pltpu.SemaphoreType.DMA((model_blocks,))],
            compiler_params=params(), name="turn", cost_estimate=cost(1, 1),
        )(in_vmem(state["act"]), in_hbm(tokens), *after())
        state.update(act_t=act_t, tok_t=tok_t, dep=done)

    def grads(which):
        by_hidden = which == "down"
        own, scale = state[which], scale_out if by_hidden else scale_in
        if by_hidden:
            left, right, peer = state["act_t"], state["err"], peer_down
        else:
            left, right, peer = state["tok_t"], state["dpre"], peer_up
        o, done = pl.pallas_call(
            functools.partial(grad_kernel, scale, by_hidden), out_shape=(like(blocks, blk, blk), token),
            in_specs=[SMEM, SMEM] + [ANYV] * 3 + [ANY] * 3, out_specs=(ANY, ANY),
            scratch_shapes=[V(*own.shape), V(*own.shape),
                            pltpu.SMEM((blocks,), jnp.int32), pltpu.SMEM((blocks // per_column,), jnp.int32),
                            pltpu.SemaphoreType.DMA((2,))],
            compiler_params=params(), name=f"grad_{which}", cost_estimate=cost(1, 1),
        )(block_rows, block_columns, in_vmem(left), in_vmem(right), in_vmem(own), in_hbm(peer), *after())
        new[which] = o
        state["dep"] = done

    order = plan()
    for what, c, j in order:
        if what == "F":
            forward(c)
        elif what == "A":
            add(c, j)
        elif what == "S":
            error(c)
        elif what == "T":
            turn()
        elif what == "X":
            state["also"] = (peer_up, peer_down)[c]
        elif what == "B":
            backward(c)
        elif what == "P":
            pass_on(c, j)
        elif what == "E":
            finish(c)
        else:
            grads(what)
    return new["up"][None], new["down"][None], state["out"]


ORDER = (
    "F0", "F1", "F2", "A02", "F3", "A12", "A03", "T0", "A22", "X0", "A13", "B0", "A32", "A23", "B1", "P02", "A33",
    "B2", "X1", "P03", "P12", "B3", "P13", "P22", "D0", "P23", "E0", "E1", "P32", "U0", "P33", "E2", "E3",
)


def plan():
    named = {"D": "down", "U": "up"}
    out = []
    for word in ORDER:
        what = word[0]
        if what in named:
            out.append((named[what], 0, 0))
        else:
            out.append((what, int(word[1]), int(word[2]) if len(word) > 2 else 0))
    return out


SHARES = (192, 192, 192, 192)
GROUPS = ((0,), (1,), (2,), (3,))
DIRECT_SUM = ()
DIRECT_GRAD = ()


def solution(mesh):
    return jax.shard_map(
        functools.partial(on_device, SHARES, GROUPS, DIRECT_SUM, DIRECT_GRAD),
        mesh=mesh,
        in_specs=(P("dp", None), P("dp", None), P("dp", "tensor", None, None), P("dp", "tensor", None, None),
                  P("tensor"), P("tensor")),
        out_specs=(P("dp", "tensor", None, None), P("dp", "tensor", None, None), P("dp", "tensor")),
        check_vma=False,
    )
```

```python
import functools

import jax
import jax.numpy as jnp
from jax import lax
from jax.experimental import pallas as pl
from jax.experimental.pallas import tpu as pltpu
from jax.sharding import PartitionSpec as P

step_rate = 0.5
per_column = 2
ANY = pl.BlockSpec(memory_space=pltpu.HBM)
ANYV = pl.BlockSpec(memory_space=pltpu.VMEM)
SMEM = pl.BlockSpec(memory_space=pltpu.SMEM)
f32 = jnp.float32
bf16 = jnp.bfloat16


def params(mib=20):
    return pltpu.CompilerParams(vmem_limit_bytes=mib << 20)


def cost(word):
    return pl.CostEstimate(flops=HEAVY.get(word, 1), bytes_accessed=1, transcendentals=0)


def lanes(index, size):
    return pl.ds(pl.multiple_of(index * size, size), size)


def column_table(cols_ref, table, count, blocks):
    for h in range(blocks // per_column):
        count[h] = 0
    for k in range(blocks):
        h = cols_ref[k]
        seen = count[h]
        table[per_column * h + seen] = k
        count[h] = seen + 1


def forward_kernel(start, scale_in, scale_out, direct, first, rows_ref, cols_ref, tok_hbm, up, down, dep, also, *refs):
    if first:
        up_hbm, down_hbm = up, down
        (part, act, fac, up, down), refs = refs[:5], refs[5:]
    else:
        (part, act, fac), refs = refs[2:5], refs[5:]
    outs, token, (tok, acc, table, count, sems), refs = refs[:direct], refs[direct], refs[direct + 1:direct + 6], refs[direct + 6:]
    size, width = tok.shape
    blocks, blk = up.shape[0], up.shape[1]
    mine = pl.ds(start, size)
    copies = [pltpu.make_async_copy(tok_hbm.at[mine], tok, sems.at[0])]
    if first:
        small = [pltpu.make_async_copy(rows_ref, refs[0], sems.at[1]), pltpu.make_async_copy(cols_ref, refs[1], sems.at[2])]
        rows_ref, cols_ref = refs
        copies += small
    for c in copies:
        c.start()
    if first:
        ups = [pltpu.make_async_copy(up_hbm.at[k], up.at[k], sems.at[3]) for k in range(blocks)]
        downs = [pltpu.make_async_copy(down_hbm.at[k], down.at[k], sems.at[4]) for k in range(blocks)]
        for c in ups + downs:
            c.start()
    acc[...] = jnp.zeros_like(acc)
    for c in copies[1:]:
        c.wait()
    column_table(cols_ref, table, count, blocks)
    copies[0].wait()
    if first:
        for c in ups:
            c.wait()
    for h in range(blocks // per_column):
        pre = None
        for j in range(per_column):
            k = table[per_column * h + j]
            term = jnp.dot(tok[:, lanes(rows_ref[k], blk)], up[k], preferred_element_type=f32)
            pre = term if pre is None else pre + term
        pre = pre * scale_in
        sig = 1.0 / (1.0 + jnp.exp(-pre))
        act[mine, h * blk:(h + 1) * blk] = (pre * sig).astype(bf16)
        fac[mine, h * blk:(h + 1) * blk] = (sig * (1.0 + pre * (1.0 - sig)) * scale_out).astype(bf16)
    if first:
        for c in downs:
            c.wait()
    for k in range(blocks):
        r = rows_ref[k]
        acc[r] += jnp.dot(act[mine, lanes(cols_ref[k], blk)], down[k], preferred_element_type=f32)
    for b in range(acc.shape[0]):
        part[:, b * blk:(b + 1) * blk] = (acc[b] * scale_out).astype(bf16)
    for c in shares_of(part, outs, sems.at[5]):
        c.wait()


def shares_of(whole, outs, sem):
    if not outs:
        return []
    share = whole.shape[1] // (len(outs) + 1)
    place = lax.axis_index("tensor")
    copies = [pltpu.make_async_copy(whole.at[:, lanes(place ^ (i + 1), share)], out, sem) for i, out in enumerate(outs)]
    for c in copies:
        c.start()
    return copies


def backward_kernel(start, sizes, terms, ready, direct, first, scale_in, rows_ref, cols_ref, *refs):
    parts, refs = refs[:terms * len(sizes)], refs[terms * len(sizes):]
    (tgt_hbm, fac, up, down, dep, also), refs = refs[:6], refs[6 if first else 8:]
    (back, send, err, dpre), outs, refs = refs[:4], refs[4:4 + direct], refs[5 + direct:]
    tgt, acc, table, count, sems = refs
    size, width = tgt.shape
    blocks, blk = up.shape[0], up.shape[1]
    mine = pl.ds(start, size)
    place = lax.axis_index("tensor")
    if not ready:
        copy = pltpu.make_async_copy(tgt_hbm.at[mine], tgt, sems.at[0])
        copy.start()
    column_table(cols_ref, table, count, blocks)
    acc[...] = jnp.zeros_like(acc)
    share = width // terms
    if ready:
        copies, offset = [], start
        for n, rows in enumerate(sizes):
            for i in range(terms):
                target = err.at[pl.ds(offset, rows), lanes(place ^ i, share)]
                copies.append(pltpu.make_async_copy(parts[n * terms + i], target, sems.at[0]))
                copies[-1].start()
            offset += rows
        for c in copies:
            c.wait()
    else:
        copy.wait()
        offset = 0
        for n, rows in enumerate(sizes):
            for b in range(width // blk):
                s = slice(b * blk, (b + 1) * blk)
                total = parts[n * terms][:, s].astype(f32)
                for i in range(1, terms):
                    total += parts[n * terms + i][:, s].astype(f32)
                err[pl.ds(start + offset, rows), s] = (total - tgt[pl.ds(offset, rows), s].astype(f32)).astype(bf16)
            offset += rows
    for h in range(blocks // per_column):
        dact = None
        for j in range(per_column):
            k = table[per_column * h + j]
            term = jnp.dot(err[mine, lanes(rows_ref[k], blk)], down[k], preferred_element_type=f32)
            dact = term if dact is None else dact + term
        s = slice(h * blk, (h + 1) * blk)
        dpre[mine, s] = (dact * fac[mine, s].astype(f32)).astype(bf16)
    for k in range(blocks):
        r = rows_ref[k]
        acc[r] += jnp.dot(dpre[mine, lanes(cols_ref[k], blk)], up[k], preferred_element_type=f32)
    for b in range(acc.shape[0]):
        back[:, b * blk:(b + 1) * blk] = (acc[b] * scale_in).astype(bf16)
    out = shares_of(back, outs, sems.at[1])
    if not direct and terms > 1:
        first_column = jnp.where(place == 0, share, 0)
        copy = pltpu.make_async_copy(back.at[:, pl.ds(pl.multiple_of(first_column, share), width - share)], send, sems.at[1])
        copy.start()
        out.append(copy)
    for c in out:
        c.wait()


def error_kernel(start, count, *refs):
    terms, (tgt_hbm, dep, also, o_ref, token, tgt, sem) = refs[:count], refs[count:]
    size, share = tgt.shape
    own = lanes(lax.axis_index("tensor"), share)
    copy = pltpu.make_async_copy(tgt_hbm.at[pl.ds(start, size), own], tgt, sem)
    copy.start()
    total = terms[0][:, own].astype(f32)
    for i in range(1, count):
        total += terms[i][...].astype(f32)
    copy.wait()
    o_ref[...] = (total - tgt[...].astype(f32)).astype(bf16)


def add_kernel(a_ref, b_ref, dep, also, o_ref, token):
    o_ref[...] = (a_ref[...].astype(f32) + b_ref[...].astype(f32)).astype(bf16)


def pass_on_kernel(hop, count, back, got, dep, also, o_ref, token):
    width = o_ref.shape[1]
    part = width // (count - hop)
    right = lax.axis_index("tensor") == hop - 1
    a = back[:, pl.ds(pl.multiple_of(jnp.where(right, hop * part, 0), part), width)]
    b = got[:, pl.ds(pl.multiple_of(jnp.where(right, part, 0), part), width)]
    o_ref[...] = (a.astype(f32) + b.astype(f32)).astype(bf16)


def finish_kernel(start, count, direct, *refs):
    terms, (old, dep, also, out_hbm, token, buf, sem) = refs[:count], refs[count:]
    size, part = buf.shape
    place = lax.axis_index("tensor")
    total = terms[0][:, lanes(place, part)].astype(f32)
    for j in range(1, count):
        if direct:
            total += terms[j][...].astype(f32)
        else:
            at = jnp.where(place == j, 0, (count - 1 - j) * part)
            total += terms[j][:, pl.ds(pl.multiple_of(at, part), part)].astype(f32)
    buf[...] = total.astype(bf16)
    copy = pltpu.make_async_copy(buf, out_hbm.at[pl.ds(start, size)], sem)
    copy.start()
    copy.wait()


def turn_kernel(act, tok_hbm, dep, also, act_t, tok_t, token, tok, sems):
    count, blk = act_t.shape[0], act_t.shape[1]
    columns = [slice(b * blk, (b + 1) * blk) for b in range(count)]
    copies = [pltpu.make_async_copy(tok_hbm.at[:, c], tok.at[:, c], sems.at[b]) for b, c in enumerate(columns)]
    for c in copies:
        c.start()
    for b, c in enumerate(columns):
        act_t[b] = act[:, c].T
    for b, c in enumerate(columns):
        copies[b].wait()
        tok_t[b] = tok[:, c].T


def turn_weights_kernel(up, down, dep, also, up_t, down_t, token):
    for k in range(up.shape[0]):
        up_t[k] = up[k].T
        down_t[k] = down[k].T


def grad_kernel(scale, by_hidden, rows_ref, cols_ref, left, right, own, peer_hbm, dep, also, out_hbm, token,
                peer, out, table, count, sems):
    blocks, blk = own.shape[0], own.shape[1]
    copies = [pltpu.make_async_copy(peer_hbm.at[k], peer.at[k], sems.at[0]) for k in range(blocks)]
    for c in copies:
        c.start()
    column_table(cols_ref, table, count, blocks)
    for c in copies:
        c.wait()
    done = []
    for h in range(blocks // per_column):
        for j in range(per_column):
            k = table[per_column * h + j]
            model = rows_ref[k]
            if by_hidden:
                grad = jnp.dot(left[h], right[:, lanes(model, blk)], preferred_element_type=f32)
            else:
                grad = jnp.dot(left[model], right[:, h * blk:(h + 1) * blk], preferred_element_type=f32)
            mixed = 0.5 * (own[k].astype(f32) + peer[k].astype(f32))
            out[k] = (mixed - (step_rate * scale) * grad).astype(bf16)
            done.append(pltpu.make_async_copy(out.at[k], out_hbm.at[k], sems.at[1]))
            done[-1].start()
    for c in done:
        c.wait()


def cut(total, shares, unit=16):
    edges = [0]
    for i in range(1, len(shares)):
        edges.append(round(total * sum(shares[:i]) / sum(shares) / unit) * unit)
    edges.append(total)
    return [(a, b - a) for a, b in zip(edges, edges[1:]) if b > a]


def on_device(shares, groups, direct_sum, direct_grad, tokens, targets, up_weight, down_weight, block_rows, block_columns):
    tok_count, width = tokens.shape
    up, down = up_weight[0], down_weight[0]
    blocks, blk = up.shape[0], up.shape[1]
    count = lax.axis_size("tensor")
    hops = count - 1
    hidden = blocks // per_column * blk
    scale_in = (width // 4) ** -0.5
    scale_out = (hidden * count // 4) ** -0.5
    level = (lax.axis_size("dp").bit_length() - 1) // 2
    part = width // count
    model_blocks = width // blk

    def hop(x, j):
        return lax.ppermute(x, "tensor", [(j - 1, j), (count - j, count - 1 - j)])

    def across(x, k):
        return lax.ppermute(x, "tensor", [(i, i ^ k) for i in range(count)])

    def partner(x):
        return lax.ppermute(x, "dp", [(i, i ^ (1 << level)) for i in range(lax.axis_size("dp"))])

    peer_up, peer_down = partner(up), partner(down)
    chunks = cut(tok_count, shares)
    C = len(chunks)
    like = lambda *s: jax.ShapeDtypeStruct(s, bf16)
    V = lambda *s: pltpu.VMEM(s, bf16)

    state = dict(act=None, fac=None, err=None, dpre=None, out=None, dep=block_rows)
    part_of, back_of, new = {}, {}, {}
    got = {}
    gotg = {}

    token = pltpu.HBM((16, 128), bf16)
    in_hbm = lambda x: pltpu.with_memory_space_constraint(x, pltpu.HBM)
    in_vmem = lambda x: pltpu.with_memory_space_constraint(x, pltpu.VMEM)
    weights = lambda: (in_vmem(state["up"]), in_vmem(state["down"]))

    spans = [(chunks[g[0]][0], sum(chunks[c][1] for c in g)) for g in groups]

    def after():
        return in_hbm(state["dep"]), in_hbm(state.pop("also", state["dep"]))

    def forward(c):
        start, size = chunks[c]
        first = c == 0
        direct = hops if c in direct_sum else 0
        scratch = [V(size, width), pltpu.VMEM((model_blocks, size, blk), f32),
                   pltpu.SMEM((blocks,), jnp.int32), pltpu.SMEM((blocks // per_column,), jnp.int32),
                   pltpu.SemaphoreType.DMA((6,))]
        held = (V(tok_count, hidden), V(tok_count, hidden))
        if first:
            scratch += [pltpu.SMEM((blocks,), jnp.int32), pltpu.SMEM((blocks,), jnp.int32)]
            a = [in_hbm(x) for x in (block_rows, block_columns, tokens, up, down, block_rows, block_rows)]
            specs, alias = [ANY] * 7, {}
            held += (V(*up.shape), V(*down.shape))
        else:
            a = [block_rows, block_columns, in_hbm(tokens), *weights(), *after(), in_vmem(state["act"]), in_vmem(state["fac"])]
            specs, alias = [SMEM, SMEM, ANY, ANYV, ANYV, ANY, ANY, ANYV, ANYV], {7: 1, 8: 2}
        p, act, fac, *outs = pl.pallas_call(
            functools.partial(forward_kernel, start, scale_in, scale_out, direct, first),
            out_shape=(V(size, width), *held) + (like(size, part),) * direct + (token,),
            in_specs=specs, out_specs=(ANYV,) * (1 + len(held) + direct) + (ANY,),
            input_output_aliases=alias, scratch_shapes=scratch,
            compiler_params=params(), name=f"forward_{c}", cost_estimate=cost(f"F{c}"),
        )(*a)
        if first:
            state.update(up=outs.pop(0), down=outs.pop(0))
        *sends, done = outs
        state.update(act=act, fac=fac, dep=done)
        part_of[c] = p
        if direct:
            for i, x in enumerate(sends):
                got[c, i + 1] = across(x, i + 1)
        elif hops:
            got[c, 1] = hop(p, 1)

    def error(c):
        start, size = chunks[c]
        e, done = pl.pallas_call(
            functools.partial(error_kernel, start, count), out_shape=(like(size, part), token),
            in_specs=[ANYV] * count + [ANY] * 3, out_specs=(ANYV, ANY),
            scratch_shapes=[V(size, part), pltpu.SemaphoreType.DMA],
            compiler_params=params(), name=f"error_{c}", cost_estimate=cost(f"S{c}"),
        )(part_of[c], *[got[c, i] for i in range(1, count)], in_hbm(targets), *after())
        state["dep"] = done
        got[c, 0] = e
        for i in range(1, count):
            got[c, i] = across(e, i)

    def add(c, j):
        start, size = chunks[c]
        s, done = pl.pallas_call(
            add_kernel, out_shape=(like(size, width), token),
            in_specs=[ANYV, ANYV, ANY, ANY], out_specs=(ANYV, ANY),
            compiler_params=params(), name=f"add_{c}_{j}", cost_estimate=cost(f"A{c}{j}"),
        )(part_of[c], got[c, j - 1], *after())
        state["dep"] = done
        got[c, j] = hop(s, j)

    def backward(c):
        start, size = spans[c]
        first = c == 0
        ready = groups[c][0] in direct_sum
        direct = hops if c in direct_grad else 0
        a = [block_rows, block_columns]
        for n in groups[c]:
            a += [got[n, 0] if ready else part_of[n]] + [got[n, j] for j in range(1, count)]
        a += [in_hbm(targets), in_vmem(state["fac"]), in_vmem(state["up_t"]), in_vmem(state["down_t"]), *after()]
        specs = [SMEM, SMEM] + [ANYV] * (count * len(groups[c])) + [ANY] + [ANYV] * 3 + [ANY] * 2
        alias = {}
        if not first:
            alias = {len(a): 2, len(a) + 1: 3}
            a += [in_vmem(state["err"]), in_vmem(state["dpre"])]
            specs += [ANYV] * 2
        chain = like(size, width - part) if hops and not direct else like(16, 128)
        g, send, err, dpre, *sends, done = pl.pallas_call(
            functools.partial(backward_kernel, start, [chunks[n][1] for n in groups[c]], count, ready, direct, first, scale_in),
            out_shape=(V(size, width), chain, V(tok_count, width), V(tok_count, hidden)) + (like(size, part),) * direct + (token,),
            in_specs=specs, out_specs=(ANYV,) * (4 + direct) + (ANY,),
            input_output_aliases=alias,
            scratch_shapes=[V(size, width), pltpu.VMEM((model_blocks, size, blk), f32),
                            pltpu.SMEM((blocks,), jnp.int32), pltpu.SMEM((blocks // per_column,), jnp.int32),
                            pltpu.SemaphoreType.DMA((2,))],
            compiler_params=params(), name=f"backward_{c}", cost_estimate=cost(f"B{c}"),
        )(*a)
        state.update(err=err, dpre=dpre, dep=done)
        back_of[c] = g
        if direct:
            for i, x in enumerate(sends):
                gotg[c, i + 1] = across(x, i + 1)
        elif hops:
            gotg[c, 1] = hop(send, 1)

    def pass_on(c, j):
        start, size = spans[c]
        wide = (count - j) * part
        s, done = pl.pallas_call(
            functools.partial(pass_on_kernel, j, count), out_shape=(like(size, wide), token),
            in_specs=[ANYV, ANYV, ANY, ANY], out_specs=(ANYV, ANY),
            compiler_params=params(), name=f"pass_on_{c}_{j}", cost_estimate=cost(f"P{c}{j}"),
        )(back_of[c], gotg[c, j - 1], *after())
        state["dep"] = done
        gotg[c, j] = hop(s, j)

    def finish(c):
        start, size = spans[c]
        first = state["out"] is None
        a = [back_of[c]] + [gotg[c, j] for j in range(1, count)] + [tokens if first else state["out"], *after()]
        o, done = pl.pallas_call(
            functools.partial(finish_kernel, start, count, c in direct_grad), out_shape=(like(tok_count, part), token),
            in_specs=[ANYV] * count + [ANY] * 3, out_specs=(ANY, ANY),
            input_output_aliases={} if first else {count: 0},
            scratch_shapes=[V(size, part), pltpu.SemaphoreType.DMA],
            compiler_params=params(), name=f"finish_{c}", cost_estimate=cost(f"E{c}"),
        )(*a)
        state.update(out=o, dep=done)

    def turn():
        turned = V(model_blocks, blk, tok_count)
        act_t, tok_t, done = pl.pallas_call(
            turn_kernel, out_shape=(turned, turned, token), in_specs=[ANYV] + [ANY] * 3, out_specs=(ANYV, ANYV, ANY),
            scratch_shapes=[V(tok_count, width), pltpu.SemaphoreType.DMA((model_blocks,))],
            compiler_params=params(), name="turn", cost_estimate=cost("T0"),
        )(in_vmem(state["act"]), in_hbm(tokens), *after())
        state.update(act_t=act_t, tok_t=tok_t, dep=done)

    def turn_weights():
        W = V(blocks, blk, blk)
        up_t, down_t, done = pl.pallas_call(
            turn_weights_kernel, out_shape=(W, W, token), in_specs=[ANYV] * 2 + [ANY] * 2, out_specs=(ANYV, ANYV, ANY),
            compiler_params=params(), name="turn_weights", cost_estimate=cost("W0"),
        )(*weights(), *after())
        state.update(up_t=up_t, down_t=down_t, dep=done)

    def grads(which):
        by_hidden = which == "down"
        own, scale = state[which], scale_out if by_hidden else scale_in
        if by_hidden:
            left, right, peer = state["act_t"], state["err"], peer_down
        else:
            left, right, peer = state["tok_t"], state["dpre"], peer_up
        o, done = pl.pallas_call(
            functools.partial(grad_kernel, scale, by_hidden), out_shape=(like(blocks, blk, blk), token),
            in_specs=[SMEM, SMEM] + [ANYV] * 3 + [ANY] * 3, out_specs=(ANY, ANY),
            scratch_shapes=[V(*own.shape), V(*own.shape),
                            pltpu.SMEM((blocks,), jnp.int32), pltpu.SMEM((blocks // per_column,), jnp.int32),
                            pltpu.SemaphoreType.DMA((2,))],
            compiler_params=params(), name=f"grad_{which}", cost_estimate=cost("D0" if by_hidden else "U0"),
        )(block_rows, block_columns, in_vmem(left), in_vmem(right), in_vmem(own), in_hbm(peer), *after())
        new[which] = o
        state["dep"] = done

    order = plan()
    for what, c, j in order:
        if what == "F":
            forward(c)
        elif what == "A":
            add(c, j)
        elif what == "S":
            error(c)
        elif what == "T":
            turn()
        elif what == "W":
            turn_weights()
        elif what == "X":
            state["also"] = (peer_up, peer_down)[c]
        elif what == "B":
            backward(c)
        elif what == "P":
            pass_on(c, j)
        elif what == "E":
            finish(c)
        else:
            grads(what)
    return new["up"][None], new["down"][None], state["out"]


ORDER = (
    "F0", "F1", "F2", "A02", "F3", "W0", "A12", "A03", "T0", "A22", "X0", "A13", "B0", "A32", "A23", "B1", "P02",
    "A33", "B2", "P03", "P12", "X1", "B3", "E0", "P13", "P22", "D0", "P23", "U0", "E3", "E1", "E2",
)


def plan():
    named = {"D": "down", "U": "up"}
    out = []
    for word in ORDER:
        what = word[0]
        if what in named:
            out.append((named[what], 0, 0))
        else:
            out.append((what, int(word[1]), int(word[2]) if len(word) > 2 else 0))
    return out


SHARES = (192, 192, 192, 192)
HEAVY = {"E1": 10000000000, "E3": 10000000000, "E2": 10000000000, "B1": 10000000000}
GROUPS = ((0,), (1,), (2,), (3,))
DIRECT_SUM = ()
DIRECT_GRAD = (3,)


def solution(mesh):
    return jax.shard_map(
        functools.partial(on_device, SHARES, GROUPS, DIRECT_SUM, DIRECT_GRAD),
        mesh=mesh,
        in_specs=(P("dp", None), P("dp", None), P("dp", "tensor", None, None), P("dp", "tensor", None, None),
                  P("tensor"), P("tensor")),
        out_specs=(P("dp", "tensor", None, None), P("dp", "tensor", None, None), P("dp", "tensor")),
        check_vma=False,
    )
```
